32 devices in a mesh: layer: 1, dp: 32 (over z, y, x, core).
Axes of the slice: x: 2, y: 2, z: 4, core: 2. Of those that a mesh axis runs over, the one named last changes fastest.
Arguments:
- activations: bfloat16 [1, 4096, 5120], P('layer', 'dp'), may hold values from -6 to 6
- out_grads: bfloat16 [1, 4096, 5120], P('layer', 'dp'), may hold values from -6 to 6
- projectors: bfloat16 [1, 5120, 128], P('layer'), may hold values from -0.078125 to 0.078125
- rewards: float32 [128], P('dp'), may hold values from -8 to 8
- lengths: int32 [128], P('dp'), may hold values from 1 to 32, 3072 in all
- pairing: int32 [64, 2], P('dp'), may hold values from 0 to 3, as said below
- queries: bfloat16 [1, 256, 4096], P('layer', 'dp'), may hold values from -0.0078125 to 0.0078125
Outputs:
- scores: float32 [64, 256], P('dp', 'layer')
The draws below stay inside these ranges and needn't reach their ends.
Inputs may be any that keep to these rules, and one draw needn't show every extreme that they name: `pairing`: the 2 pairs of one dp index name each of that index's 2 * 2 sequences exactly once.
All inputs are finite; a program needn't handle non-finite values. No bound on the sum of `lengths` on one device may be relied on, other than what follows from the above.
Results may differ from the reference program's by a relative error of at most 0.0029.
Values may be sent and summed in bfloat16 or wider, within the bound.
A program may use at most 64 MiB of HBM per device.

```python
import math
import jax
import jax.numpy as jnp
import numpy as np
from jax import lax

D = 5120
K = 64
PAIR_DEV = 2
LEN = 32
PROJS = 1
PAIRS = 64
SEQS = 128
TOKENS = 4096
QUERIES = 256


def draw_pairing(key, part):
    key = jax.random.fold_in(key, 11)
    blocks = PAIRS // PAIR_DEV
    subkeys = jax.random.split(key, blocks)
    orders = jax.vmap(lambda subkey: jax.random.permutation(subkey, 2 * PAIR_DEV))(subkeys)
    return orders.reshape(PAIRS, 2).astype(jnp.int32)


def levels(stream_key, extent, cuts, least, high):
    gain = 1.0
    for dim, shards_of in cuts:
        draws = jax.random.uniform(jax.random.fold_in(jax.random.fold_in(stream_key, 6), dim), (shards_of,), jnp.float32, least / len(cuts), high / len(cuts))
        gain = gain * jnp.repeat(jnp.exp(draws), extent[dim] // shards_of).reshape((-1,) + (1,) * (len(extent) - 1 - dim))
    return gain


def profile(number_of, total, reach, slope):
    portions = [(1 << 20) // math.isqrt(rank ** slope) + 1 for rank in range(2, number_of + 1)]
    rest, given = total - reach - (number_of - 1), [1] * (number_of - 1)
    while rest > 0:
        free = [i for i in range(number_of - 1) if given[i] < reach]
        pool, remaining = sum([portions[i] for i in free]), rest
        for i in free:
            extra = min(reach - given[i], max(1, remaining * portions[i] // pool), rest)
            given[i] = given[i] + extra
            rest = rest - extra
    return np.array([reach] + given)


def ragged_sizes(own_key, amount, total, most, slope):
    if amount == 2:
        one = jax.random.randint(own_key, (), max(1, total - most), min(most, total - 1) + 1)
        return jnp.stack([one, total - one])
    sizes = jnp.asarray(profile(amount, total, most, slope), jnp.int32)
    pairs = (amount - 1) // 2
    source_of, receiver = sizes[1:1 + 2 * pairs:2], sizes[2:2 + 2 * pairs:2]
    room = jnp.minimum(source_of - 1, most - receiver)
    shifted = jax.random.randint(jax.random.fold_in(own_key, 1), (pairs,), 0, 1 << 20) % (room + 1)
    sizes = sizes.at[1:1 + 2 * pairs:2].set(source_of - shifted).at[2:2 + 2 * pairs:2].set(receiver + shifted)
    return sizes[jax.random.permutation(jax.random.fold_in(own_key, 2), amount)]


def noise(key, shape, spread, limit, pieces=(), kind=jnp.bfloat16):
    loudness = levels(key, shape, pieces, -0.22, 0.18) if pieces else 1.0
    result = jax.random.normal(key, shape, jnp.float32) * spread * loudness
    return jnp.minimum(jnp.maximum(result, -limit), limit).astype(kind)


def setup_inputs(seed: int = 0) -> dict:
    seeds = jax.random.split(jax.random.key(seed), 8)
    return {
        "activations": noise(seeds[0], (PROJS, TOKENS, D), 1.0, 6.0, ((1, 32),)),
        "out_grads": noise(seeds[1], (PROJS, TOKENS, D), 1.0, 6.0, ((1, 32),)),
        "projectors": noise(seeds[2], (PROJS, D, 2 * K), D ** -0.5, 0.078125),
        "rewards": noise(seeds[3], (SEQS,), 2.0, 8.0, ((0, 32),), jnp.float32),
        "lengths": ragged_sizes(seeds[4], SEQS, (3 * SEQS * LEN) // 4, LEN, 1).astype(jnp.int32),
        "pairing": draw_pairing(jax.random.fold_in(seeds[7], 71), 0),
        "queries": noise(seeds[6], (PROJS, QUERIES, K * K), (4 * K * K * LEN) ** -0.5, 0.0078125, ((1, 32),)),
    }


def reference(activations, out_grads, projectors, rewards, lengths, pairing, queries):
    places = jnp.arange(LEN, dtype=jnp.int32)
    live_mask = (places[None, :] < lengths[:, None]).astype(jnp.float32)
    offsets = (jnp.arange(PAIRS, dtype=jnp.int32) // PAIR_DEV) * (2 * PAIR_DEV)
    chosen = offsets + pairing[:, 0]
    rejected = offsets + pairing[:, 1]
    margin_weight = 1.0 - jax.nn.sigmoid(rewards[chosen] - rewards[rejected])
    scores = jnp.zeros((PAIRS, QUERIES), jnp.float32)
    for index in range(projectors.shape[0]):
        proj_act = jnp.dot(activations[index], projectors[index, :, :K], preferred_element_type=jnp.float32)
        proj_grad = jnp.dot(out_grads[index], projectors[index, :, K:], preferred_element_type=jnp.float32)
        grad_rows = proj_grad.reshape(SEQS, LEN, K) * live_mask[:, :, None]
        act_rows = proj_act.reshape(SEQS, LEN, K)
        seq_grads = jnp.einsum("stk,stj->skj", grad_rows, act_rows, precision=lax.Precision.HIGHEST).reshape(SEQS, K * K)
        train_grads = (margin_weight[:, None] * (seq_grads[rejected] - seq_grads[chosen])).astype(jnp.bfloat16)
        scores = scores + jnp.dot(train_grads, queries[index].T, preferred_element_type=jnp.float32)
    return scores
```

```python
import functools
import math

import jax
import jax.numpy as jnp
from jax import lax
from jax.experimental import pallas as pl
from jax.experimental.pallas import tpu as pltpu
from jax.sharding import PartitionSpec as P

LANES = 128
CHUNKS = 4


def kernel(
    outer, reps, inner,
    act_ref, grad_ref, proj_ref, rewards_ref, lengths_ref, pairing_ref, queries_ref, out_ref,
    tokens, weights, query_all, outer_products, train_send, train_recv, part_send, part_recv,
    load_sem, own_sem, q1_send, q1_recv, q2_send, q2_recv, t_send, t_recv, p_send, p_recv,
):
    group = outer * inner
    me = lax.axis_index("dp")
    place = me % inner
    rep = (me // inner) % reps
    slab = me // (inner * reps)
    mine = slab * inner + place
    slots, width = act_ref.shape[1], act_ref.shape[2]
    seq_count = lengths_ref.shape[0]
    seq_len = slots // seq_count
    half = proj_ref.shape[2] // 2
    pair_count = pairing_ref.shape[0]
    entries = queries_ref.shape[2] // group
    rows = entries // LANES

    def member(step):
        other = (mine + step) % group
        return other, (other // inner * reps + rep) * inner + other % inner

    def twin(step):
        return (slab * reps + (rep + step) % reps) * inner + place

    part = width // CHUNKS
    loads = []
    for c in range(CHUNKS):
        cols = pl.ds(c * part, part)
        loads.append([
            pltpu.make_async_copy(proj_ref.at[0, cols, :], weights.at[cols, :], load_sem.at[c, 0]),
            pltpu.make_async_copy(
                act_ref.at[0, :, cols], tokens.at[pl.ds(0, slots), cols], load_sem.at[c, 1]
            ),
            pltpu.make_async_copy(
                grad_ref.at[0, :, cols], tokens.at[pl.ds(slots, slots), cols], load_sem.at[c, 2]
            ),
        ])
        for copy in loads[-1]:
            copy.start()

    def chunk_of(index):
        return queries_ref.at[0, :, pl.ds(pl.multiple_of(index * entries, LANES), entries)]

    own = pltpu.make_async_copy(chunk_of(mine), query_all.at[slab, rep, place], own_sem)
    own.start()

    barrier = pltpu.get_barrier_semaphore()
    for step in range(1, group):
        pl.semaphore_signal(
            barrier, inc=1, device_id={"dp": member(step)[1]}, device_id_type=pl.DeviceIdType.MESH
        )
    for step in range(1, reps):
        pl.semaphore_signal(
            barrier, inc=1, device_id={"dp": twin(step)}, device_id_type=pl.DeviceIdType.MESH
        )
    pl.semaphore_wait(barrier, group - 1 + reps - 1)

    def send(src, dst, send_sem, recv_sem, device):
        copy = pltpu.make_async_remote_copy(
            src_ref=src, dst_ref=dst, send_sem=send_sem, recv_sem=recv_sem,
            device_id={"dp": device}, device_id_type=pl.DeviceIdType.MESH,
        )
        copy.start()
        return copy

    first = []
    for step in range(1, group):
        other, device = member(step)
        first.append(send(
            chunk_of(other), query_all.at[slab, rep, place], q1_send.at[step], q1_recv.at[step], device
        ))

    lane = lax.broadcasted_iota(jnp.int32, (seq_len, LANES), 1)
    spot = lax.broadcasted_iota(jnp.int32, (seq_len, LANES), 0)
    signs = []
    for s in range(seq_count):
        sign = []
        for i in range(pair_count):
            is_chosen = (pairing_ref[i, 0] == s).astype(jnp.float32)
            is_rejected = (pairing_ref[i, 1] == s).astype(jnp.float32)
            sign.append(is_rejected - is_chosen)
        both = jnp.where(lane < half, sign[0], sign[1])
        signs.append(jnp.where(spot < lengths_ref[s], both, 0.0))
    signs = jnp.concatenate(signs, axis=0)
    pair_weights = []
    for i in range(pair_count):
        margin = jnp.float32(0.0)
        for s in range(seq_count):
            reward = rewards_ref[s]
            margin = margin + jnp.where(pairing_ref[i, 0] == s, reward, 0.0)
            margin = margin - jnp.where(pairing_ref[i, 1] == s, reward, 0.0)
        pair_weights.append(1.0 - jax.nn.sigmoid(jnp.full((half, LANES), margin, jnp.float32)))

    projected = jnp.zeros((2 * slots, 2 * half), jnp.float32)
    for c in range(CHUNKS):
        for copy in loads[c]:
            copy.wait()
        cols = pl.ds(c * part, part)
        projected += jnp.dot(tokens[:, cols], weights[cols, :], preferred_element_type=jnp.float32)

    own.wait()
    for copy in first:
        copy.wait()
    second = [
        send(
            query_all.at[:, rep], query_all.at[:, rep], q2_send.at[step], q2_recv.at[step], twin(step)
        )
        for step in range(1, reps)
    ]

    token_lane = lax.broadcasted_iota(jnp.int32, (slots, LANES), 1)
    act = projected[:slots]
    act = jnp.where(token_lane < half, act, pltpu.roll(act, half, 1))
    grad = projected[slots:]
    grad = jnp.where(token_lane < half, pltpu.roll(grad, half, 1), grad)
    products = lax.dot_general(
        grad * signs, act, (((0,), (0,)), ((), ())),
        precision=lax.Precision.HIGHEST, preferred_element_type=jnp.float32,
    )
    outer_products[...] = products * jnp.concatenate(pair_weights, axis=0)
    lines = pair_count * half // 2
    even = outer_products[pl.ds(0, lines, stride=2), :]
    odd = outer_products[pl.ds(1, lines, stride=2), :]
    flat_lane = lax.broadcasted_iota(jnp.int32, (lines, LANES), 1)
    flat = jnp.where(flat_lane < half, even, odd)
    for g in range(group):
        for i in range(pair_count):
            start = i * (half // 2) + g * rows
            train_send[g, i * rows:(i + 1) * rows, :] = flat[start:start + rows]
    train_recv[mine] = train_send[mine]
    train_copies = []
    for step in range(1, group):
        other, device = member(step)
        train_copies.append(send(
            train_send.at[other], train_recv.at[mine], t_send.at[step], t_recv.at[step], device
        ))

    for copy in second:
        copy.wait()
    query_rows = query_all[...].astype(jnp.float32).reshape(-1, entries).astype(jnp.bfloat16)
    for copy in train_copies:
        copy.wait()

    received = train_recv[...].reshape(group * pair_count, rows, LANES)
    left = jnp.concatenate([received[:, r, :] for r in range(rows)], axis=1).astype(jnp.bfloat16)
    partial = lax.dot_general(
        left, query_rows, (((1,), (1,)), ((), ())), preferred_element_type=jnp.float32
    )
    for g in range(group):
        part_send[g] = partial[g * pair_count:(g + 1) * pair_count]
    part_recv[mine] = part_send[mine]
    part_copies = []
    for step in range(1, group):
        other, device = member(step)
        part_copies.append(send(
            part_send.at[other], part_recv.at[mine], p_send.at[step], p_recv.at[step], device
        ))
    for copy in part_copies:
        copy.wait()
    total = part_recv[0]
    for g in range(1, group):
        total += part_recv[g]
    out_ref[...] = total


def solution(mesh):
    devices = mesh.shape["dp"]
    inner = math.gcd(devices, 2)
    outer = math.gcd(devices // inner, 4)
    reps = devices // (inner * outer)
    group = outer * inner

    def local(activations, out_grads, projectors, rewards, lengths, pairing, queries):
        slots, width = activations.shape[1:]
        half = projectors.shape[2] // 2
        pair_count = pairing.shape[0]
        per_device, length = queries.shape[1:]
        entries = length // group
        rows = pair_count * entries // LANES
        dma = lambda *shape: pltpu.SemaphoreType.DMA(shape)
        smem = pl.BlockSpec(memory_space=pltpu.SMEM)
        hbm = pl.BlockSpec(memory_space=pl.ANY)
        partial_scores = pl.pallas_call(
            functools.partial(kernel, outer, reps, inner),
            out_shape=jax.ShapeDtypeStruct((pair_count, devices * per_device), jnp.float32),
            in_specs=[hbm, hbm, hbm, smem, smem, smem, hbm],
            out_specs=pl.BlockSpec(memory_space=pltpu.VMEM),
            scratch_shapes=[
                pltpu.VMEM((2 * slots, width), jnp.bfloat16),
                pltpu.VMEM((width, 2 * half), jnp.bfloat16),
                pltpu.VMEM((outer, reps, inner, per_device, entries), jnp.bfloat16),
                pltpu.VMEM((pair_count * half, LANES), jnp.float32),
                pltpu.VMEM((group, rows, LANES), jnp.float32),
                pltpu.VMEM((group, rows, LANES), jnp.float32),
                pltpu.VMEM((group, pair_count, devices * per_device), jnp.float32),
                pltpu.VMEM((group, pair_count, devices * per_device), jnp.float32),
                dma(CHUNKS, 3), dma(), dma(group), dma(group), dma(reps), dma(reps),
                dma(group), dma(group), dma(group), dma(group),
            ],
            compiler_params=pltpu.CompilerParams(
                collective_id=0, has_side_effects=True, vmem_limit_bytes=40 * 1024 * 1024
            ),
        )(activations, out_grads, projectors, rewards, lengths, pairing, queries)
        return lax.psum_scatter(partial_scores, "layer", scatter_dimension=1, tiled=True)

    return jax.shard_map(
        local,
        mesh=mesh,
        in_specs=(
            P("layer", "dp", None),
            P("layer", "dp", None),
            P("layer", None, None),
            P("dp"),
            P("dp"),
            P("dp", None),
            P("layer", "dp", None),
        ),
        out_specs=P("dp", "layer"),
        check_vma=False,
    )
```

```python
import functools
import math

import jax
import jax.numpy as jnp
from jax import lax
from jax.experimental import pallas as pl
from jax.experimental.pallas import tpu as pltpu
from jax.sharding import PartitionSpec as P

LANES = 128
CHUNKS = 4


def kernel(
    outer, reps, inner,
    act_ref, grad_ref, proj_ref, rewards_hbm, lengths_hbm, pairing_hbm, queries_ref, out_ref,
    tokens, weights, query_all, outer_products, train_send, train_recv, part_send, part_recv,
    rewards_ref, lengths_ref, pairing_ref, small_sem, load_sem, own_sem, q1_send, q1_recv, q2_send, q2_recv, t_send, t_recv, p_send, p_recv,
):
    group = outer * inner
    me = lax.axis_index("dp")
    place = me % inner
    rep = (me // inner) % reps
    slab = me // (inner * reps)
    mine = slab * inner + place
    slots, width = act_ref.shape[1], act_ref.shape[2]
    seq_count = lengths_hbm.shape[0]
    seq_len = slots // seq_count
    half = proj_ref.shape[2] // 2
    pair_count = pairing_hbm.shape[0]
    entries = queries_ref.shape[2] // group
    rows = entries // LANES

    def member(step):
        other = (mine + step) % group
        return other, (other // inner * reps + rep) * inner + other % inner

    def twin(step):
        return (slab * reps + (rep + step) % reps) * inner + place

    part = width // CHUNKS
    loads = []
    for c in range(CHUNKS):
        cols = pl.ds(c * part, part)
        loads.append([
            pltpu.make_async_copy(proj_ref.at[0, cols, :], weights.at[cols, :], load_sem.at[c, 0]),
            pltpu.make_async_copy(
                act_ref.at[0, :, cols], tokens.at[pl.ds(0, slots), cols], load_sem.at[c, 1]
            ),
            pltpu.make_async_copy(
                grad_ref.at[0, :, cols], tokens.at[pl.ds(slots, slots), cols], load_sem.at[c, 2]
            ),
        ])
        for copy in loads[-1]:
            copy.start()

    def chunk_of(index):
        return queries_ref.at[0, :, pl.ds(pl.multiple_of(index * entries, LANES), entries)]

    own = pltpu.make_async_copy(chunk_of(mine), query_all.at[slab, rep, place], own_sem)
    own.start()
    small = [
        pltpu.make_async_copy(rewards_hbm, rewards_ref, small_sem.at[0]),
        pltpu.make_async_copy(lengths_hbm, lengths_ref, small_sem.at[1]),
        pltpu.make_async_copy(pairing_hbm, pairing_ref, small_sem.at[2]),
    ]
    for copy in small:
        copy.start()

    barrier = pltpu.get_barrier_semaphore()
    for step in range(1, group):
        pl.semaphore_signal(
            barrier, inc=1, device_id={"dp": member(step)[1]}, device_id_type=pl.DeviceIdType.MESH
        )
    for step in range(1, reps):
        pl.semaphore_signal(
            barrier, inc=1, device_id={"dp": twin(step)}, device_id_type=pl.DeviceIdType.MESH
        )
    pl.semaphore_wait(barrier, group - 1 + reps - 1)

    def send(src, dst, send_sem, recv_sem, device):
        copy = pltpu.make_async_remote_copy(
            src_ref=src, dst_ref=dst, send_sem=send_sem, recv_sem=recv_sem,
            device_id={"dp": device}, device_id_type=pl.DeviceIdType.MESH,
        )
        copy.start()
        return copy

    first = []
    for step in range(1, group):
        other, device = member(step)
        first.append(send(
            chunk_of(other), query_all.at[slab, rep, place], q1_send.at[step], q1_recv.at[step], device
        ))

    for copy in small:
        copy.wait()
    lane = lax.broadcasted_iota(jnp.int32, (seq_len, LANES), 1)
    spot = lax.broadcasted_iota(jnp.int32, (seq_len, LANES), 0)
    signs = []
    for s in range(seq_count):
        sign = []
        for i in range(pair_count):
            is_chosen = (pairing_ref[i, 0] == s).astype(jnp.float32)
            is_rejected = (pairing_ref[i, 1] == s).astype(jnp.float32)
            sign.append(is_rejected - is_chosen)
        both = jnp.where(lane < half, sign[0], sign[1])
        signs.append(jnp.where(spot < lengths_ref[s], both, 0.0))
    signs = jnp.concatenate(signs, axis=0)
    pair_weights = []
    for i in range(pair_count):
        margin = jnp.float32(0.0)
        for s in range(seq_count):
            reward = rewards_ref[s]
            margin = margin + jnp.where(pairing_ref[i, 0] == s, reward, 0.0)
            margin = margin - jnp.where(pairing_ref[i, 1] == s, reward, 0.0)
        pair_weights.append(1.0 - jax.nn.sigmoid(jnp.full((half, LANES), margin, jnp.float32)))

    projected = jnp.zeros((2 * slots, 2 * half), jnp.float32)
    for c in range(CHUNKS):
        for copy in loads[c]:
            copy.wait()
        cols = pl.ds(c * part, part)
        projected += jnp.dot(tokens[:, cols], weights[cols, :], preferred_element_type=jnp.float32)

    own.wait()
    for copy in first:
        copy.wait()
    second = [
        send(
            query_all.at[:, rep], query_all.at[:, rep], q2_send.at[step], q2_recv.at[step], twin(step)
        )
        for step in range(1, reps)
    ]

    token_lane = lax.broadcasted_iota(jnp.int32, (slots, LANES), 1)
    act = projected[:slots]
    act = jnp.where(token_lane < half, act, pltpu.roll(act, half, 1))
    grad = projected[slots:]
    grad = jnp.where(token_lane < half, pltpu.roll(grad, half, 1), grad)
    products = lax.dot_general(
        grad * signs, act, (((0,), (0,)), ((), ())),
        precision=lax.Precision.HIGHEST, preferred_element_type=jnp.float32,
    )
    outer_products[...] = products * jnp.concatenate(pair_weights, axis=0)
    lines = pair_count * half // 2
    even = outer_products[pl.ds(0, lines, stride=2), :]
    odd = outer_products[pl.ds(1, lines, stride=2), :]
    flat_lane = lax.broadcasted_iota(jnp.int32, (lines, LANES), 1)
    flat = jnp.where(flat_lane < half, even, odd)
    for g in range(group):
        for i in range(pair_count):
            start = i * (half // 2) + g * rows
            train_send[g, i * rows:(i + 1) * rows, :] = flat[start:start + rows]
    train_recv[mine] = train_send[mine]
    train_copies = []
    for step in range(1, group):
        other, device = member(step)
        train_copies.append(send(
            train_send.at[other], train_recv.at[mine], t_send.at[step], t_recv.at[step], device
        ))

    for copy in second:
        copy.wait()
    query_rows = query_all[...].astype(jnp.float32).reshape(-1, entries).astype(jnp.bfloat16)
    for copy in train_copies:
        copy.wait()

    received = train_recv[...].reshape(group * pair_count, rows, LANES)
    left = jnp.concatenate([received[:, r, :] for r in range(rows)], axis=1).astype(jnp.bfloat16)
    partial = lax.dot_general(
        left, query_rows, (((1,), (1,)), ((), ())), preferred_element_type=jnp.float32
    )
    for g in range(group):
        part_send[g] = partial[g * pair_count:(g + 1) * pair_count]
    part_recv[mine] = part_send[mine]
    part_copies = []
    for step in range(1, group):
        other, device = member(step)
        part_copies.append(send(
            part_send.at[other], part_recv.at[mine], p_send.at[step], p_recv.at[step], device
        ))
    for copy in part_copies:
        copy.wait()
    total = part_recv[0]
    for g in range(1, group):
        total += part_recv[g]
    out_ref[...] = total


def solution(mesh):
    devices = mesh.shape["dp"]
    inner = math.gcd(devices, 2)
    outer = math.gcd(devices // inner, 4)
    reps = devices // (inner * outer)
    group = outer * inner

    def local(activations, out_grads, projectors, rewards, lengths, pairing, queries):
        slots, width = activations.shape[1:]
        half = projectors.shape[2] // 2
        pair_count = pairing.shape[0]
        per_device, length = queries.shape[1:]
        entries = length // group
        rows = pair_count * entries // LANES
        dma = lambda *shape: pltpu.SemaphoreType.DMA(shape)
        hbm = pl.BlockSpec(memory_space=pltpu.HBM)
        partial_scores = pl.pallas_call(
            functools.partial(kernel, outer, reps, inner),
            out_shape=jax.ShapeDtypeStruct((pair_count, devices * per_device), jnp.float32),
            in_specs=[hbm] * 7,
            out_specs=pl.BlockSpec(memory_space=pltpu.VMEM),
            scratch_shapes=[
                pltpu.VMEM((2 * slots, width), jnp.bfloat16),
                pltpu.VMEM((width, 2 * half), jnp.bfloat16),
                pltpu.VMEM((outer, reps, inner, per_device, entries), jnp.bfloat16),
                pltpu.VMEM((pair_count * half, LANES), jnp.float32),
                pltpu.VMEM((group, rows, LANES), jnp.float32),
                pltpu.VMEM((group, rows, LANES), jnp.float32),
                pltpu.VMEM((group, pair_count, devices * per_device), jnp.float32),
                pltpu.VMEM((group, pair_count, devices * per_device), jnp.float32),
                pltpu.SMEM(rewards.shape, rewards.dtype),
                pltpu.SMEM(lengths.shape, lengths.dtype),
                pltpu.SMEM(pairing.shape, pairing.dtype),
                dma(3), dma(CHUNKS, 3), dma(), dma(group), dma(group), dma(reps), dma(reps),
                dma(group), dma(group), dma(group), dma(group),
            ],
            compiler_params=pltpu.CompilerParams(
                collective_id=0, has_side_effects=True, vmem_limit_bytes=56 * 1024 * 1024
            ),
        )(activations, out_grads, projectors, rewards, lengths, pairing, queries)
        return lax.psum_scatter(partial_scores, "layer", scatter_dimension=1, tiled=True)

    return jax.shard_map(
        local,
        mesh=mesh,
        in_specs=(
            P("layer", "dp", None),
            P("layer", "dp", None),
            P("layer", None, None),
            P("dp"),
            P("dp"),
            P("dp", None),
            P("layer", "dp", None),
        ),
        out_specs=P("dp", "layer"),
        check_vma=False,
    )
```

```python
import functools
import math

import jax
import jax.numpy as jnp
from jax import lax
from jax.experimental import pallas as pl
from jax.experimental.pallas import tpu as pltpu
from jax.sharding import PartitionSpec as P

LANES = 128
CHUNKS = 4


def kernel(
    outer, reps, inner,
    act_ref, grad_ref, proj_ref, rewards_hbm, lengths_hbm, pairing_hbm, queries_ref, out_ref,
    tokens, weights, query_all, outer_products, train_send, train_recv, part_send, part_recv,
    rewards_ref, lengths_ref, pairing_ref, small_sem, load_sem, own_sem, q1_send, q1_recv, q2_send, q2_recv, t_send, t_recv, p_send, p_recv,
):
    group = outer * inner
    me = lax.axis_index("dp")
    place = me % inner
    rep = (me // inner) % reps
    slab = me // (inner * reps)
    mine = slab * inner + place
    slots, width = act_ref.shape[1], act_ref.shape[2]
    seq_count = lengths_hbm.shape[0]
    seq_len = slots // seq_count
    half = proj_ref.shape[2] // 2
    pair_count = pairing_hbm.shape[0]
    entries = queries_ref.shape[2] // group
    rows = entries // LANES

    def member(step):
        other = lax.rem(mine + step, group)
        return other, (other // inner * reps + rep) * inner + lax.rem(other, inner)

    def twin(step):
        return (slab * reps + lax.rem(rep + step, reps)) * inner + place

    def repeat(low, high, body):
        lax.fori_loop(low, high, lambda step, carry: (body(step), carry)[1], 0)

    part = width // CHUNKS

    def loads(c):
        cols = pl.ds(pl.multiple_of(c * part, LANES), part)
        return (
            pltpu.make_async_copy(proj_ref.at[0, cols, :], weights.at[c], load_sem.at[c, 0]),
            pltpu.make_async_copy(
                act_ref.at[0, :, cols], tokens.at[c, pl.ds(0, slots), :], load_sem.at[c, 1]
            ),
            pltpu.make_async_copy(
                grad_ref.at[0, :, cols], tokens.at[c, pl.ds(slots, slots), :], load_sem.at[c, 2]
            ),
        )

    def start_loads(c):
        for copy in loads(c):
            copy.start()

    barrier = pltpu.get_barrier_semaphore()

    def greet(device):
        pl.semaphore_signal(
            barrier, inc=1, device_id={"dp": device}, device_id_type=pl.DeviceIdType.MESH
        )

    repeat(1, group, lambda step: greet(member(step)[1]))
    repeat(1, reps, lambda step: greet(twin(step)))
    repeat(0, CHUNKS, start_loads)

    def chunk_of(index):
        return queries_ref.at[0, :, pl.ds(pl.multiple_of(index * entries, LANES), entries)]

    own = pltpu.make_async_copy(chunk_of(mine), query_all.at[slab, rep, place], own_sem)
    own.start()
    small = [
        pltpu.make_async_copy(rewards_hbm, rewards_ref, small_sem.at[0]),
        pltpu.make_async_copy(lengths_hbm, lengths_ref, small_sem.at[1]),
        pltpu.make_async_copy(pairing_hbm, pairing_ref, small_sem.at[2]),
    ]
    for copy in small:
        copy.start()
    pl.semaphore_wait(barrier, group - 1 + reps - 1)

    def remote(src, dst, send_sem, recv_sem, device):
        return pltpu.make_async_remote_copy(
            src_ref=src, dst_ref=dst, send_sem=send_sem, recv_sem=recv_sem,
            device_id={"dp": device}, device_id_type=pl.DeviceIdType.MESH,
        )

    def first(step):
        other, device = member(step)
        return remote(
            chunk_of(other), query_all.at[slab, rep, place], q1_send.at[step], q1_recv.at[step], device
        )

    repeat(1, group, lambda step: first(step).start())

    for copy in small:
        copy.wait()
    lane = lax.broadcasted_iota(jnp.int32, (seq_len, LANES), 1)
    spot = lax.broadcasted_iota(jnp.int32, (seq_len, LANES), 0)
    signs = []
    for s in range(seq_count):
        sign = []
        for i in range(pair_count):
            is_chosen = (pairing_ref[i, 0] == s).astype(jnp.float32)
            is_rejected = (pairing_ref[i, 1] == s).astype(jnp.float32)
            sign.append(is_rejected - is_chosen)
        both = jnp.where(lane < half, sign[0], sign[1])
        signs.append(jnp.where(spot < lengths_ref[s], both, 0.0))
    signs = jnp.concatenate(signs, axis=0)
    pair_weights = []
    for i in range(pair_count):
        margin = jnp.float32(0.0)
        for s in range(seq_count):
            reward = rewards_ref[s]
            margin = margin + jnp.where(pairing_ref[i, 0] == s, reward, 0.0)
            margin = margin - jnp.where(pairing_ref[i, 1] == s, reward, 0.0)
        pair_weights.append(1.0 - jax.nn.sigmoid(jnp.full((1, LANES), margin, jnp.float32)))

    def project(c, total):
        for copy in loads(c):
            copy.wait()
        return total + jnp.dot(tokens[c], weights[c], preferred_element_type=jnp.float32)

    projected = lax.fori_loop(
        0, CHUNKS, project, jnp.zeros((2 * slots, 2 * half), jnp.float32)
    )

    def second(step):
        mates = query_all.at[:, rep]
        return remote(mates, mates, q2_send.at[step], q2_recv.at[step], twin(step))

    own.wait()
    repeat(1, group, lambda step: first(step).wait())
    repeat(1, reps, lambda step: second(step).start())

    token_lane = lax.broadcasted_iota(jnp.int32, (slots, LANES), 1)
    act = projected[:slots]
    act = jnp.where(token_lane < half, act, pltpu.roll(act, half, 1))
    grad = projected[slots:]
    grad = jnp.where(token_lane < half, pltpu.roll(grad, half, 1), grad)
    products = lax.dot_general(
        grad * signs, act, (((0,), (0,)), ((), ())),
        precision=lax.Precision.HIGHEST, preferred_element_type=jnp.float32,
    )
    for i in range(pair_count):
        outer_products[i * half:(i + 1) * half, :] = products[i * half:(i + 1) * half] * pair_weights[i]
    lines = pair_count * half // 2
    even = outer_products[pl.ds(0, lines, stride=2), :]
    odd = outer_products[pl.ds(1, lines, stride=2), :]
    flat_lane = lax.broadcasted_iota(jnp.int32, (lines, LANES), 1)
    flat = jnp.where(flat_lane < half, even, odd)
    for g in range(group):
        for i in range(pair_count):
            start = i * (half // 2) + g * rows
            train_send[g, i * rows:(i + 1) * rows, :] = flat[start:start + rows]

    def train(step):
        other, device = member(step)
        return remote(
            train_send.at[other], train_recv.at[mine], t_send.at[step], t_recv.at[step], device
        )

    repeat(1, group, lambda step: train(step).start())
    train_recv[mine] = train_send[mine]

    repeat(1, reps, lambda step: second(step).wait())
    query_rows = query_all[...].astype(jnp.float32).reshape(-1, entries).astype(jnp.bfloat16)
    repeat(1, group, lambda step: train(step).wait())

    received = train_recv[...].reshape(group * pair_count, rows, LANES)
    left = jnp.concatenate([received[:, r, :] for r in range(rows)], axis=1).astype(jnp.bfloat16)
    partial = lax.dot_general(
        left, query_rows, (((1,), (1,)), ((), ())), preferred_element_type=jnp.float32
    )
    for g in range(group):
        part_send[g] = partial[g * pair_count:(g + 1) * pair_count]

    def scores(step):
        other, device = member(step)
        return remote(
            part_send.at[other], part_recv.at[mine], p_send.at[step], p_recv.at[step], device
        )

    repeat(1, group, lambda step: scores(step).start())
    part_recv[mine] = part_send[mine]
    repeat(1, group, lambda step: scores(step).wait())
    total = part_recv[0]
    for g in range(1, group):
        total += part_recv[g]
    out_ref[...] = total


def solution(mesh):
    devices = mesh.shape["dp"]
    inner = math.gcd(devices, 2)
    outer = math.gcd(devices // inner, 4)
    reps = devices // (inner * outer)
    group = outer * inner

    def local(activations, out_grads, projectors, rewards, lengths, pairing, queries):
        slots, width = activations.shape[1:]
        half = projectors.shape[2] // 2
        pair_count = pairing.shape[0]
        per_device, length = queries.shape[1:]
        entries = length // group
        rows = pair_count * entries // LANES
        dma = lambda *shape: pltpu.SemaphoreType.DMA(shape)
        hbm = pl.BlockSpec(memory_space=pltpu.HBM)
        partial_scores = pl.pallas_call(
            functools.partial(kernel, outer, reps, inner),
            out_shape=jax.ShapeDtypeStruct((pair_count, devices * per_device), jnp.float32),
            in_specs=[hbm] * 7,
            out_specs=pl.BlockSpec(memory_space=pltpu.VMEM),
            scratch_shapes=[
                pltpu.VMEM((CHUNKS, 2 * slots, width // CHUNKS), jnp.bfloat16),
                pltpu.VMEM((CHUNKS, width // CHUNKS, 2 * half), jnp.bfloat16),
                pltpu.VMEM((outer, reps, inner, per_device, entries), jnp.bfloat16),
                pltpu.VMEM((pair_count * half, LANES), jnp.float32),
                pltpu.VMEM((group, rows, LANES), jnp.float32),
                pltpu.VMEM((group, rows, LANES), jnp.float32),
                pltpu.VMEM((group, pair_count, devices * per_device), jnp.float32),
                pltpu.VMEM((group, pair_count, devices * per_device), jnp.float32),
                pltpu.SMEM(rewards.shape, rewards.dtype),
                pltpu.SMEM(lengths.shape, lengths.dtype),
                pltpu.SMEM(pairing.shape, pairing.dtype),
                dma(3), dma(CHUNKS, 3), dma(), dma(group), dma(group), dma(reps), dma(reps),
                dma(group), dma(group), dma(group), dma(group),
            ],
            compiler_params=pltpu.CompilerParams(
                collective_id=0, has_side_effects=True, vmem_limit_bytes=56 * 1024 * 1024
            ),
        )(activations, out_grads, projectors, rewards, lengths, pairing, queries)
        return lax.psum_scatter(partial_scores, "layer", scatter_dimension=1, tiled=True)

    return jax.shard_map(
        local,
        mesh=mesh,
        in_specs=(
            P("layer", "dp", None),
            P("layer", "dp", None),
            P("layer", None, None),
            P("dp"),
            P("dp"),
            P("dp", None),
            P("layer", "dp", None),
        ),
        out_specs=P("dp", "layer"),
        check_vma=False,
    )
```

```python
import functools
import math

import jax
import jax.numpy as jnp
from jax import lax
from jax.experimental import pallas as pl
from jax.experimental.pallas import tpu as pltpu
from jax.sharding import PartitionSpec as P

LANES = 128
CHUNKS = 4


def kernel(
    outer, reps, inner,
    act_ref, grad_ref, proj_ref, rewards_hbm, lengths_hbm, pairing_hbm, queries_ref, out_ref,
    tokens, weights, query_all, outer_products, train_send, train_recv, part_send, part_recv,
    rewards_ref, lengths_ref, pairing_ref, small_sem, load_sem, own_sem, q1_send, q1_recv, q2_send, q2_recv, t_send, t_recv, p_send, p_recv,
):
    group = outer * inner
    me = lax.axis_index("dp")
    place = me % inner
    rep = (me // inner) % reps
    slab = me // (inner * reps)
    mine = slab * inner + place
    slots, width = act_ref.shape[1], act_ref.shape[2]
    seq_count = lengths_hbm.shape[0]
    seq_len = slots // seq_count
    half = proj_ref.shape[2] // 2
    pair_count = pairing_hbm.shape[0]
    entries = queries_ref.shape[2] // group
    rows = entries // LANES

    def member(step):
        other = lax.rem(mine + step, group)
        return other, (other // inner * reps + rep) * inner + lax.rem(other, inner)

    def twin(step):
        return (slab * reps + lax.rem(rep + step, reps)) * inner + place

    def repeat(low, high, body):
        lax.fori_loop(low, high, lambda step, carry: (body(step), carry)[1], 0)

    part = width // CHUNKS

    def loads(c):
        cols = pl.ds(pl.multiple_of(c * part, LANES), part)
        return (
            pltpu.make_async_copy(proj_ref.at[0, cols, :], weights.at[c], load_sem.at[c, 0]),
            pltpu.make_async_copy(
                act_ref.at[0, :, cols], tokens.at[c, pl.ds(0, slots), :], load_sem.at[c, 1]
            ),
            pltpu.make_async_copy(
                grad_ref.at[0, :, cols], tokens.at[c, pl.ds(slots, slots), :], load_sem.at[c, 2]
            ),
        )

    def start_loads(c):
        for copy in loads(c):
            copy.start()

    barrier = pltpu.get_barrier_semaphore()

    def greet(device):
        pl.semaphore_signal(
            barrier, inc=1, device_id={"dp": device}, device_id_type=pl.DeviceIdType.MESH
        )

    repeat(1, group, lambda step: greet(member(step)[1]))
    repeat(1, reps, lambda step: greet(twin(step)))
    repeat(0, CHUNKS, start_loads)

    def chunk_of(index):
        return queries_ref.at[0, :, pl.ds(pl.multiple_of(index * entries, LANES), entries)]

    own = pltpu.make_async_copy(chunk_of(mine), query_all.at[slab, rep, place], own_sem)
    own.start()
    small = [
        pltpu.make_async_copy(rewards_hbm, rewards_ref, small_sem.at[0]),
        pltpu.make_async_copy(lengths_hbm, lengths_ref, small_sem.at[1]),
        pltpu.make_async_copy(pairing_hbm, pairing_ref, small_sem.at[2]),
    ]
    for copy in small:
        copy.start()
    pl.semaphore_wait(barrier, group - 1 + reps - 1)

    def remote(src, dst, send_sem, recv_sem, device):
        return pltpu.make_async_remote_copy(
            src_ref=src, dst_ref=dst, send_sem=send_sem, recv_sem=recv_sem,
            device_id={"dp": device}, device_id_type=pl.DeviceIdType.MESH,
        )

    def first(step):
        other, device = member(step)
        return remote(
            chunk_of(other), query_all.at[slab, rep, place], q1_send.at[step], q1_recv.at[step], device
        )

    repeat(1, group, lambda step: first(step).start())

    for copy in small:
        copy.wait()
    lane = lax.broadcasted_iota(jnp.int32, (seq_len, LANES), 1)
    spot = lax.broadcasted_iota(jnp.int32, (seq_len, LANES), 0)
    signs = []
    for s in range(seq_count):
        sign = []
        for i in range(pair_count):
            is_chosen = (pairing_ref[i, 0] == s).astype(jnp.float32)
            is_rejected = (pairing_ref[i, 1] == s).astype(jnp.float32)
            sign.append(is_rejected - is_chosen)
        both = jnp.where(lane < half, sign[0], sign[1])
        signs.append(jnp.where(spot < lengths_ref[s], both, 0.0))
    signs = jnp.concatenate(signs, axis=0)
    pair_weights = []
    for i in range(pair_count):
        margin = jnp.float32(0.0)
        for s in range(seq_count):
            reward = rewards_ref[s]
            margin = margin + jnp.where(pairing_ref[i, 0] == s, reward, 0.0)
            margin = margin - jnp.where(pairing_ref[i, 1] == s, reward, 0.0)
        pair_weights.append(1.0 - jax.nn.sigmoid(jnp.full((1, LANES), margin, jnp.float32)))

    def project(c, total):
        for copy in loads(c):
            copy.wait()
        return total + jnp.dot(tokens[c], weights[c], preferred_element_type=jnp.float32)

    projected = lax.fori_loop(
        0, CHUNKS, project, jnp.zeros((2 * slots, 2 * half), jnp.float32)
    )

    def second(step):
        mates = query_all.at[:, rep]
        return remote(mates, mates, q2_send.at[step], q2_recv.at[step], twin(step))

    own.wait()
    repeat(1, group, lambda step: first(step).wait())
    repeat(1, reps, lambda step: second(step).start())

    token_lane = lax.broadcasted_iota(jnp.int32, (slots, LANES), 1)
    act = projected[:slots]
    act = jnp.where(token_lane < half, act, pltpu.roll(act, half, 1))
    grad = projected[slots:]
    grad = jnp.where(token_lane < half, pltpu.roll(grad, half, 1), grad)
    products = lax.dot_general(
        grad * signs, act, (((0,), (0,)), ((), ())),
        precision=lax.Precision.HIGHEST, preferred_element_type=jnp.float32,
    )
    for i in range(pair_count):
        outer_products[i * half:(i + 1) * half, :] = products[i * half:(i + 1) * half] * pair_weights[i]
    lines = pair_count * half // 2
    even = outer_products[pl.ds(0, lines, stride=2), :]
    odd = outer_products[pl.ds(1, lines, stride=2), :]
    flat_lane = lax.broadcasted_iota(jnp.int32, (lines, LANES), 1)
    flat = jnp.where(flat_lane < half, even, odd)
    for g in range(group):
        for i in range(pair_count):
            start = i * (half // 2) + g * rows
            train_send[g, i * rows:(i + 1) * rows, :] = flat[start:start + rows]

    def train(step):
        other, device = member(step)
        return remote(
            train_send.at[other], train_recv.at[mine], t_send.at[step], t_recv.at[step], device
        )

    repeat(1, group, lambda step: train(step).start())
    train_recv[mine] = train_send[mine]

    repeat(1, reps, lambda step: second(step).wait())
    query_rows = query_all[...].astype(jnp.float32).reshape(-1, entries).astype(jnp.bfloat16)
    repeat(1, group, lambda step: train(step).wait())

    received = train_recv[...].reshape(group * pair_count, rows, LANES)
    left = jnp.concatenate([received[:, r, :] for r in range(rows)], axis=1).astype(jnp.bfloat16)
    partial = lax.dot_general(
        left, query_rows, (((1,), (1,)), ((), ())), preferred_element_type=jnp.float32
    )
    for g in range(group):
        part_send[g] = partial[g * pair_count:(g + 1) * pair_count]

    def scores(step):
        other, device = member(step)
        return remote(
            part_send.at[other], part_recv.at[mine], p_send.at[step], p_recv.at[step], device
        )

    repeat(1, group, lambda step: scores(step).start())
    part_recv[mine] = part_send[mine]
    repeat(1, group, lambda step: scores(step).wait())
    total = part_recv[0]
    for g in range(1, group):
        total += part_recv[g]
    out_ref[...] = total


def solution(mesh):
    devices = mesh.shape["dp"]
    inner = 1
    outer = math.gcd(devices, 16)
    reps = devices // (inner * outer)
    group = outer * inner

    def local(activations, out_grads, projectors, rewards, lengths, pairing, queries):
        slots, width = activations.shape[1:]
        half = projectors.shape[2] // 2
        pair_count = pairing.shape[0]
        per_device, length = queries.shape[1:]
        entries = length // group
        rows = pair_count * entries // LANES
        dma = lambda *shape: pltpu.SemaphoreType.DMA(shape)
        hbm = pl.BlockSpec(memory_space=pltpu.HBM)
        partial_scores = pl.pallas_call(
            functools.partial(kernel, outer, reps, inner),
            out_shape=jax.ShapeDtypeStruct((pair_count, devices * per_device), jnp.float32),
            in_specs=[hbm] * 7,
            out_specs=pl.BlockSpec(memory_space=pltpu.VMEM),
            scratch_shapes=[
                pltpu.VMEM((CHUNKS, 2 * slots, width // CHUNKS), jnp.bfloat16),
                pltpu.VMEM((CHUNKS, width // CHUNKS, 2 * half), jnp.bfloat16),
                pltpu.VMEM((outer, reps, inner, per_device, entries), jnp.bfloat16),
                pltpu.VMEM((pair_count * half, LANES), jnp.float32),
                pltpu.VMEM((group, rows, LANES), jnp.float32),
                pltpu.VMEM((group, rows, LANES), jnp.float32),
                pltpu.VMEM((group, pair_count, devices * per_device), jnp.float32),
                pltpu.VMEM((group, pair_count, devices * per_device), jnp.float32),
                pltpu.SMEM(rewards.shape, rewards.dtype),
                pltpu.SMEM(lengths.shape, lengths.dtype),
                pltpu.SMEM(pairing.shape, pairing.dtype),
                dma(3), dma(CHUNKS, 3), dma(), dma(group), dma(group), dma(reps), dma(reps),
                dma(group), dma(group), dma(group), dma(group),
            ],
            compiler_params=pltpu.CompilerParams(
                collective_id=0, has_side_effects=True, vmem_limit_bytes=56 * 1024 * 1024
            ),
        )(activations, out_grads, projectors, rewards, lengths, pairing, queries)
        return lax.psum_scatter(partial_scores, "layer", scatter_dimension=1, tiled=True)

    return jax.shard_map(
        local,
        mesh=mesh,
        in_specs=(
            P("layer", "dp", None),
            P("layer", "dp", None),
            P("layer", None, None),
            P("dp"),
            P("dp"),
            P("dp", None),
            P("layer", "dp", None),
        ),
        out_specs=P("dp", "layer"),
        check_vma=False,
    )
```

```python
import functools
import math

import jax
import jax.numpy as jnp
from jax import lax
from jax.experimental import pallas as pl
from jax.experimental.pallas import tpu as pltpu
from jax.sharding import PartitionSpec as P

LANES = 128
CHUNKS = 4


def kernel(
    outer, reps, inner,
    act_ref, grad_ref, proj_ref, rewards_hbm, lengths_hbm, pairing_hbm, queries_ref, out_ref,
    tokens, weights, query_all, outer_products, train_send, train_recv, part_send, part_recv,
    rewards_ref, lengths_ref, pairing_ref, small_sem, load_sem, own_sem, q_send, q_recv, t_send, t_recv, p_send, p_recv,
):
    group = outer * inner
    me = lax.axis_index("dp")
    place = me % inner
    rep = (me // inner) % reps
    slab = me // (inner * reps)
    mine = slab * inner + place
    slots, width = act_ref.shape[1], act_ref.shape[2]
    seq_count = lengths_hbm.shape[0]
    seq_len = slots // seq_count
    half = proj_ref.shape[2] // 2
    pair_count = pairing_hbm.shape[0]
    entries = queries_ref.shape[2] // group
    rows = entries // LANES

    def member(step):
        other = lax.rem(mine + step, group)
        return other, (other // inner * reps + rep) * inner + lax.rem(other, inner)

    def stranger(step):
        device = lax.rem(me + step, outer * reps * inner)
        return device // (inner * reps) * inner + lax.rem(device, inner), device

    def repeat(low, high, body):
        lax.fori_loop(low, high, lambda step, carry: (body(step), carry)[1], 0)

    part = width // CHUNKS

    def loads(c):
        cols = pl.ds(pl.multiple_of(c * part, LANES), part)
        return (
            pltpu.make_async_copy(proj_ref.at[0, cols, :], weights.at[c], load_sem.at[c, 0]),
            pltpu.make_async_copy(
                act_ref.at[0, :, cols], tokens.at[c, pl.ds(0, slots), :], load_sem.at[c, 1]
            ),
            pltpu.make_async_copy(
                grad_ref.at[0, :, cols], tokens.at[c, pl.ds(slots, slots), :], load_sem.at[c, 2]
            ),
        )

    def start_loads(c):
        for copy in loads(c):
            copy.start()

    barrier = pltpu.get_barrier_semaphore()

    def greet(device):
        pl.semaphore_signal(
            barrier, inc=1, device_id={"dp": device}, device_id_type=pl.DeviceIdType.MESH
        )

    devices = outer * reps * inner
    repeat(0, CHUNKS, start_loads)
    repeat(1, devices, lambda step: greet(stranger(step)[1]))

    def chunk_of(index):
        return queries_ref.at[0, :, pl.ds(pl.multiple_of(index * entries, LANES), entries)]

    own = pltpu.make_async_copy(chunk_of(mine), query_all.at[me], own_sem)
    own.start()
    small = [
        pltpu.make_async_copy(rewards_hbm, rewards_ref, small_sem.at[0]),
        pltpu.make_async_copy(lengths_hbm, lengths_ref, small_sem.at[1]),
        pltpu.make_async_copy(pairing_hbm, pairing_ref, small_sem.at[2]),
    ]
    for copy in small:
        copy.start()
    pl.semaphore_wait(barrier, devices - 1)

    def remote(src, dst, send_sem, recv_sem, device):
        return pltpu.make_async_remote_copy(
            src_ref=src, dst_ref=dst, send_sem=send_sem, recv_sem=recv_sem,
            device_id={"dp": device}, device_id_type=pl.DeviceIdType.MESH,
        )

    def query(step):
        other, device = stranger(step)
        return remote(
            chunk_of(other), query_all.at[me], q_send.at[step], q_recv.at[step], device
        )

    repeat(1, devices, lambda step: query(step).start())

    for copy in small:
        copy.wait()
    lane = lax.broadcasted_iota(jnp.int32, (seq_len, LANES), 1)
    spot = lax.broadcasted_iota(jnp.int32, (seq_len, LANES), 0)
    signs = []
    for s in range(seq_count):
        sign = []
        for i in range(pair_count):
            is_chosen = (pairing_ref[i, 0] == s).astype(jnp.float32)
            is_rejected = (pairing_ref[i, 1] == s).astype(jnp.float32)
            sign.append(is_rejected - is_chosen)
        both = jnp.where(lane < half, sign[0], sign[1])
        signs.append(jnp.where(spot < lengths_ref[s], both, 0.0))
    signs = jnp.concatenate(signs, axis=0)
    pair_weights = []
    for i in range(pair_count):
        margin = jnp.float32(0.0)
        for s in range(seq_count):
            reward = rewards_ref[s]
            margin = margin + jnp.where(pairing_ref[i, 0] == s, reward, 0.0)
            margin = margin - jnp.where(pairing_ref[i, 1] == s, reward, 0.0)
        pair_weights.append(1.0 - jax.nn.sigmoid(jnp.full((1, LANES), margin, jnp.float32)))

    def project(c, total):
        for copy in loads(c):
            copy.wait()
        return total + jnp.dot(tokens[c], weights[c], preferred_element_type=jnp.float32)

    projected = lax.fori_loop(
        0, CHUNKS, project, jnp.zeros((2 * slots, 2 * half), jnp.float32)
    )

    token_lane = lax.broadcasted_iota(jnp.int32, (slots, LANES), 1)
    act = projected[:slots]
    act = jnp.where(token_lane < half, act, pltpu.roll(act, half, 1))
    grad = projected[slots:]
    grad = jnp.where(token_lane < half, pltpu.roll(grad, half, 1), grad)
    products = lax.dot_general(
        grad * signs, act, (((0,), (0,)), ((), ())),
        precision=lax.Precision.HIGHEST, preferred_element_type=jnp.float32,
    )
    for i in range(pair_count):
        outer_products[i * half:(i + 1) * half, :] = products[i * half:(i + 1) * half] * pair_weights[i]
    lines = pair_count * half // 2
    even = outer_products[pl.ds(0, lines, stride=2), :]
    odd = outer_products[pl.ds(1, lines, stride=2), :]
    flat_lane = lax.broadcasted_iota(jnp.int32, (lines, LANES), 1)
    flat = jnp.where(flat_lane < half, even, odd)
    for g in range(group):
        for i in range(pair_count):
            start = i * (half // 2) + g * rows
            train_send[g, i * rows:(i + 1) * rows, :] = flat[start:start + rows]

    def train(step):
        other, device = member(step)
        return remote(
            train_send.at[other], train_recv.at[mine], t_send.at[step], t_recv.at[step], device
        )

    repeat(1, group, lambda step: train(step).start())
    train_recv[mine] = train_send[mine]

    own.wait()
    repeat(1, devices, lambda step: query(step).wait())
    query_rows = query_all[...].astype(jnp.float32).reshape(-1, entries).astype(jnp.bfloat16)
    repeat(1, group, lambda step: train(step).wait())

    received = train_recv[...].reshape(group * pair_count, rows, LANES)
    left = jnp.concatenate([received[:, r, :] for r in range(rows)], axis=1).astype(jnp.bfloat16)
    partial = lax.dot_general(
        left, query_rows, (((1,), (1,)), ((), ())), preferred_element_type=jnp.float32
    )
    for g in range(group):
        part_send[g] = partial[g * pair_count:(g + 1) * pair_count]

    def scores(step):
        other, device = member(step)
        return remote(
            part_send.at[other], part_recv.at[mine], p_send.at[step], p_recv.at[step], device
        )

    repeat(1, group, lambda step: scores(step).start())
    part_recv[mine] = part_send[mine]
    repeat(1, group, lambda step: scores(step).wait())
    total = part_recv[0]
    for g in range(1, group):
        total += part_recv[g]
    out_ref[...] = total


def solution(mesh):
    devices = mesh.shape["dp"]
    inner = math.gcd(devices, 8)
    outer = 1
    reps = devices // (inner * outer)
    group = outer * inner

    def local(activations, out_grads, projectors, rewards, lengths, pairing, queries):
        slots, width = activations.shape[1:]
        half = projectors.shape[2] // 2
        pair_count = pairing.shape[0]
        per_device, length = queries.shape[1:]
        entries = length // group
        rows = pair_count * entries // LANES
        dma = lambda *shape: pltpu.SemaphoreType.DMA(shape)
        hbm = pl.BlockSpec(memory_space=pltpu.HBM)
        partial_scores = pl.pallas_call(
            functools.partial(kernel, outer, reps, inner),
            out_shape=jax.ShapeDtypeStruct((pair_count, devices * per_device), jnp.float32),
            in_specs=[hbm] * 7,
            out_specs=pl.BlockSpec(memory_space=pltpu.VMEM),
            scratch_shapes=[
                pltpu.VMEM((CHUNKS, 2 * slots, width // CHUNKS), jnp.bfloat16),
                pltpu.VMEM((CHUNKS, width // CHUNKS, 2 * half), jnp.bfloat16),
                pltpu.VMEM((devices, per_device, entries), jnp.bfloat16),
                pltpu.VMEM((pair_count * half, LANES), jnp.float32),
                pltpu.VMEM((group, rows, LANES), jnp.float32),
                pltpu.VMEM((group, rows, LANES), jnp.float32),
                pltpu.VMEM((group, pair_count, devices * per_device), jnp.float32),
                pltpu.VMEM((group, pair_count, devices * per_device), jnp.float32),
                pltpu.SMEM(rewards.shape, rewards.dtype),
                pltpu.SMEM(lengths.shape, lengths.dtype),
                pltpu.SMEM(pairing.shape, pairing.dtype),
                dma(3), dma(CHUNKS, 3), dma(), dma(devices), dma(devices),
                dma(group), dma(group), dma(group), dma(group),
            ],
            compiler_params=pltpu.CompilerParams(
                collective_id=0, has_side_effects=True, vmem_limit_bytes=56 * 1024 * 1024
            ),
        )(activations, out_grads, projectors, rewards, lengths, pairing, queries)
        return lax.psum_scatter(partial_scores, "layer", scatter_dimension=1, tiled=True)

    return jax.shard_map(
        local,
        mesh=mesh,
        in_specs=(
            P("layer", "dp", None),
            P("layer", "dp", None),
            P("layer", None, None),
            P("dp"),
            P("dp"),
            P("dp", None),
            P("layer", "dp", None),
        ),
        out_specs=P("dp", "layer"),
        check_vma=False,
    )
```

```python
import functools
import math

import jax
import jax.numpy as jnp
from jax import lax
from jax.experimental import pallas as pl
from jax.experimental.pallas import tpu as pltpu
from jax.sharding import PartitionSpec as P

LANES = 128
CHUNKS = 4


def kernel(
    outer, reps, inner,
    act_ref, grad_ref, proj_ref, rewards_hbm, lengths_hbm, pairing_hbm, queries_ref, out_ref,
    tokens, weights, query_all, outer_products, train_send, train_recv, part_send, part_recv,
    rewards_ref, lengths_ref, pairing_ref, small_sem, load_sem, own_sem, q_send, q_recv, t_send, t_recv, p_send, p_recv,
):
    group = outer * inner
    me = lax.axis_index("dp")
    place = me % inner
    rep = (me // inner) % reps
    slab = me // (inner * reps)
    mine = slab * inner + place
    slots, width = act_ref.shape[1], act_ref.shape[2]
    seq_count = lengths_hbm.shape[0]
    seq_len = slots // seq_count
    half = proj_ref.shape[2] // 2
    pair_count = pairing_hbm.shape[0]
    entries = queries_ref.shape[2] // group
    rows = entries // LANES

    def member(step):
        other = lax.rem(mine + step, group)
        return other, (other // inner * reps + rep) * inner + lax.rem(other, inner)

    def stranger(step):
        device = lax.rem(me + step, outer * reps * inner)
        return device // (inner * reps) * inner + lax.rem(device, inner), device

    def repeat(low, high, body):
        lax.fori_loop(low, high, lambda step, carry: (body(step), carry)[1], 0)

    part = width // CHUNKS

    def loads(c):
        cols = pl.ds(pl.multiple_of(c * part, LANES), part)
        return (
            pltpu.make_async_copy(proj_ref.at[0, cols, :], weights.at[c], load_sem.at[c, 0]),
            pltpu.make_async_copy(
                act_ref.at[0, :, cols], tokens.at[c, pl.ds(0, slots), :], load_sem.at[c, 1]
            ),
            pltpu.make_async_copy(
                grad_ref.at[0, :, cols], tokens.at[c, pl.ds(slots, slots), :], load_sem.at[c, 2]
            ),
        )

    def start_loads(c):
        for copy in loads(c):
            copy.start()

    barrier = pltpu.get_barrier_semaphore()

    def greet(device):
        pl.semaphore_signal(
            barrier, inc=1, device_id={"dp": device}, device_id_type=pl.DeviceIdType.MESH
        )

    devices = outer * reps * inner
    repeat(0, CHUNKS, start_loads)
    repeat(1, devices, lambda step: greet(stranger(step)[1]))

    def chunk_of(index):
        return queries_ref.at[0, :, pl.ds(pl.multiple_of(index * entries, LANES), entries)]

    own = pltpu.make_async_copy(chunk_of(mine), query_all.at[me], own_sem)
    own.start()
    small = [
        pltpu.make_async_copy(rewards_hbm, rewards_ref, small_sem.at[0]),
        pltpu.make_async_copy(lengths_hbm, lengths_ref, small_sem.at[1]),
        pltpu.make_async_copy(pairing_hbm, pairing_ref, small_sem.at[2]),
    ]
    for copy in small:
        copy.start()
    pl.semaphore_wait(barrier, devices - 1)

    def remote(src, dst, send_sem, recv_sem, device):
        return pltpu.make_async_remote_copy(
            src_ref=src, dst_ref=dst, send_sem=send_sem, recv_sem=recv_sem,
            device_id={"dp": device}, device_id_type=pl.DeviceIdType.MESH,
        )

    def all_of(ref, send_sem, recv_sem):
        blocks = ref.at[pl.ds(0, ref.shape[0] - 1)]
        return remote(blocks, blocks, send_sem, recv_sem, stranger(1)[1])

    def query(step):
        other, device = stranger(step)
        return remote(
            chunk_of(other), query_all.at[me], q_send, q_recv, device
        )

    repeat(1, devices, lambda step: query(step).start())

    for copy in small:
        copy.wait()
    lane = lax.broadcasted_iota(jnp.int32, (seq_len, LANES), 1)
    spot = lax.broadcasted_iota(jnp.int32, (seq_len, LANES), 0)
    signs = []
    for s in range(seq_count):
        sign = []
        for i in range(pair_count):
            is_chosen = (pairing_ref[i, 0] == s).astype(jnp.float32)
            is_rejected = (pairing_ref[i, 1] == s).astype(jnp.float32)
            sign.append(is_rejected - is_chosen)
        both = jnp.where(lane < half, sign[0], sign[1])
        signs.append(jnp.where(spot < lengths_ref[s], both, 0.0))
    signs = jnp.concatenate(signs, axis=0)
    pair_weights = []
    for i in range(pair_count):
        margin = jnp.float32(0.0)
        for s in range(seq_count):
            reward = rewards_ref[s]
            margin = margin + jnp.where(pairing_ref[i, 0] == s, reward, 0.0)
            margin = margin - jnp.where(pairing_ref[i, 1] == s, reward, 0.0)
        pair_weights.append(1.0 - jax.nn.sigmoid(jnp.full((1, LANES), margin, jnp.float32)))

    def project(c, total):
        for copy in loads(c):
            copy.wait()
        return total + jnp.dot(tokens[c], weights[c], preferred_element_type=jnp.float32)

    projected = lax.fori_loop(
        0, CHUNKS, project, jnp.zeros((2 * slots, 2 * half), jnp.float32)
    )

    token_lane = lax.broadcasted_iota(jnp.int32, (slots, LANES), 1)
    act = projected[:slots]
    act = jnp.where(token_lane < half, act, pltpu.roll(act, half, 1))
    grad = projected[slots:]
    grad = jnp.where(token_lane < half, pltpu.roll(grad, half, 1), grad)
    products = lax.dot_general(
        grad * signs, act, (((0,), (0,)), ((), ())),
        precision=lax.Precision.HIGHEST, preferred_element_type=jnp.float32,
    )
    for i in range(pair_count):
        outer_products[i * half:(i + 1) * half, :] = products[i * half:(i + 1) * half] * pair_weights[i]
    lines = pair_count * half // 2
    even = outer_products[pl.ds(0, lines, stride=2), :]
    odd = outer_products[pl.ds(1, lines, stride=2), :]
    flat_lane = lax.broadcasted_iota(jnp.int32, (lines, LANES), 1)
    flat = jnp.where(flat_lane < half, even, odd)
    for g in range(group):
        for i in range(pair_count):
            start = i * (half // 2) + g * rows
            train_send[g, i * rows:(i + 1) * rows, :] = flat[start:start + rows]

    def train(step):
        other, device = member(step)
        return remote(
            train_send.at[other], train_recv.at[mine], t_send, t_recv, device
        )

    repeat(1, group, lambda step: train(step).start())
    train_recv[mine] = train_send[mine]

    own.wait()
    queries_sent = all_of(query_all, q_send, q_recv)
    queries_sent.wait_recv()
    query_rows = query_all[...].astype(jnp.float32).reshape(-1, entries).astype(jnp.bfloat16)
    train_sent = all_of(train_recv, t_send, t_recv)
    train_sent.wait_recv()

    received = train_recv[...].reshape(group * pair_count, rows, LANES)
    left = jnp.concatenate([received[:, r, :] for r in range(rows)], axis=1).astype(jnp.bfloat16)
    partial = lax.dot_general(
        left, query_rows, (((1,), (1,)), ((), ())), preferred_element_type=jnp.float32
    )
    for g in range(group):
        part_send[g] = partial[g * pair_count:(g + 1) * pair_count]

    def scores(step):
        other, device = member(step)
        return remote(
            part_send.at[other], part_recv.at[mine], p_send, p_recv, device
        )

    repeat(1, group, lambda step: scores(step).start())
    part_recv[mine] = part_send[mine]
    scores_sent = all_of(part_recv, p_send, p_recv)
    queries_sent.wait_send()
    train_sent.wait_send()
    scores_sent.wait_send()
    scores_sent.wait_recv()
    total = part_recv[0]
    for g in range(1, group):
        total += part_recv[g]
    out_ref[...] = total


def solution(mesh):
    devices = mesh.shape["dp"]
    inner = math.gcd(devices, 8)
    outer = 1
    reps = devices // (inner * outer)
    group = outer * inner

    def local(activations, out_grads, projectors, rewards, lengths, pairing, queries):
        slots, width = activations.shape[1:]
        half = projectors.shape[2] // 2
        pair_count = pairing.shape[0]
        per_device, length = queries.shape[1:]
        entries = length // group
        rows = pair_count * entries // LANES
        dma = lambda *shape: pltpu.SemaphoreType.DMA(shape) if shape else pltpu.SemaphoreType.DMA
        hbm = pl.BlockSpec(memory_space=pltpu.HBM)
        partial_scores = pl.pallas_call(
            functools.partial(kernel, outer, reps, inner),
            out_shape=jax.ShapeDtypeStruct((pair_count, devices * per_device), jnp.float32),
            in_specs=[hbm] * 7,
            out_specs=pl.BlockSpec(memory_space=pltpu.VMEM),
            scratch_shapes=[
                pltpu.VMEM((CHUNKS, 2 * slots, width // CHUNKS), jnp.bfloat16),
                pltpu.VMEM((CHUNKS, width // CHUNKS, 2 * half), jnp.bfloat16),
                pltpu.VMEM((devices, per_device, entries), jnp.bfloat16),
                pltpu.VMEM((pair_count * half, LANES), jnp.float32),
                pltpu.VMEM((group, rows, LANES), jnp.float32),
                pltpu.VMEM((group, rows, LANES), jnp.float32),
                pltpu.VMEM((group, pair_count, devices * per_device), jnp.float32),
                pltpu.VMEM((group, pair_count, devices * per_device), jnp.float32),
                pltpu.SMEM(rewards.shape, rewards.dtype),
                pltpu.SMEM(lengths.shape, lengths.dtype),
                pltpu.SMEM(pairing.shape, pairing.dtype),
                dma(3), dma(CHUNKS, 3), dma(), dma(), dma(), dma(), dma(), dma(), dma(),
            ],
            compiler_params=pltpu.CompilerParams(
                collective_id=0, has_side_effects=True, vmem_limit_bytes=56 * 1024 * 1024
            ),
        )(activations, out_grads, projectors, rewards, lengths, pairing, queries)
        return lax.psum_scatter(partial_scores, "layer", scatter_dimension=1, tiled=True)

    return jax.shard_map(
        local,
        mesh=mesh,
        in_specs=(
            P("layer", "dp", None),
            P("layer", "dp", None),
            P("layer", None, None),
            P("dp"),
            P("dp"),
            P("dp", None),
            P("layer", "dp", None),
        ),
        out_specs=P("dp", "layer"),
        check_vma=False,
    )
```

```python
import functools
import math

import jax
import jax.numpy as jnp
from jax import lax
from jax.experimental import pallas as pl
from jax.experimental.pallas import tpu as pltpu
from jax.sharding import PartitionSpec as P

LANES = 128
CHUNKS = 4


def kernel(
    outer, reps, inner,
    act_ref, grad_ref, proj_ref, rewards_hbm, lengths_hbm, pairing_hbm, queries_ref, part_recv,
    tokens, weights, query_all, outer_products, train_send, train_recv, part_send,
    rewards_ref, lengths_ref, pairing_ref, small_sem, load_sem, own_sem, q_send, q_recv, t_send, t_recv, p_send, p_recv,
):
    group = outer * inner
    me = lax.axis_index("dp")
    place = me % inner
    rep = (me // inner) % reps
    slab = me // (inner * reps)
    mine = slab * inner + place
    slots, width = act_ref.shape[1], act_ref.shape[2]
    seq_count = lengths_hbm.shape[0]
    seq_len = slots // seq_count
    half = proj_ref.shape[2] // 2
    pair_count = pairing_hbm.shape[0]
    entries = queries_ref.shape[2] // group
    rows = entries // LANES

    def member(step):
        other = lax.rem(mine + step, group)
        return other, (other // inner * reps + rep) * inner + lax.rem(other, inner)

    def stranger(step):
        device = lax.rem(me + step, outer * reps * inner)
        return device // (inner * reps) * inner + lax.rem(device, inner), device

    def repeat(low, high, body):
        lax.fori_loop(low, high, lambda step, carry: (body(step), carry)[1], 0)

    part = width // CHUNKS

    def loads(c):
        cols = pl.ds(pl.multiple_of(c * part, LANES), part)
        return (
            pltpu.make_async_copy(proj_ref.at[0, cols, :], weights.at[c], load_sem.at[c, 0]),
            pltpu.make_async_copy(
                act_ref.at[0, :, cols], tokens.at[c, pl.ds(0, slots), :], load_sem.at[c, 1]
            ),
            pltpu.make_async_copy(
                grad_ref.at[0, :, cols], tokens.at[c, pl.ds(slots, slots), :], load_sem.at[c, 2]
            ),
        )

    def start_loads(c):
        for copy in loads(c):
            copy.start()

    barrier = pltpu.get_barrier_semaphore()

    def greet(device):
        pl.semaphore_signal(
            barrier, inc=1, device_id={"dp": device}, device_id_type=pl.DeviceIdType.MESH
        )

    devices = outer * reps * inner
    repeat(0, CHUNKS, start_loads)
    repeat(1, devices, lambda step: greet(stranger(step)[1]))

    def chunk_of(index):
        return queries_ref.at[0, :, pl.ds(pl.multiple_of(index * entries, LANES), entries)]

    own = pltpu.make_async_copy(chunk_of(mine), query_all.at[me], own_sem)
    own.start()
    small = [
        pltpu.make_async_copy(rewards_hbm, rewards_ref, small_sem.at[0]),
        pltpu.make_async_copy(lengths_hbm, lengths_ref, small_sem.at[1]),
        pltpu.make_async_copy(pairing_hbm, pairing_ref, small_sem.at[2]),
    ]
    for copy in small:
        copy.start()
    pl.semaphore_wait(barrier, devices - 1)

    def remote(src, dst, send_sem, recv_sem, device):
        return pltpu.make_async_remote_copy(
            src_ref=src, dst_ref=dst, send_sem=send_sem, recv_sem=recv_sem,
            device_id={"dp": device}, device_id_type=pl.DeviceIdType.MESH,
        )

    def all_of(ref, send_sem, recv_sem):
        blocks = ref.at[pl.ds(0, ref.shape[0] - 1)]
        return remote(blocks, blocks, send_sem, recv_sem, stranger(1)[1])

    def query(step):
        other, device = stranger(step)
        return remote(
            chunk_of(other), query_all.at[me], q_send, q_recv, device
        )

    repeat(1, devices, lambda step: query(step).start())

    for copy in small:
        copy.wait()
    lane = lax.broadcasted_iota(jnp.int32, (seq_len, LANES), 1)
    spot = lax.broadcasted_iota(jnp.int32, (seq_len, LANES), 0)
    signs = []
    for s in range(seq_count):
        sign = []
        for i in range(pair_count):
            is_chosen = (pairing_ref[i, 0] == s).astype(jnp.float32)
            is_rejected = (pairing_ref[i, 1] == s).astype(jnp.float32)
            sign.append(is_rejected - is_chosen)
        both = jnp.where(lane < half, sign[0], sign[1])
        signs.append(jnp.where(spot < lengths_ref[s], both, 0.0))
    signs = jnp.concatenate(signs, axis=0)
    pair_weights = []
    for i in range(pair_count):
        margin = jnp.float32(0.0)
        for s in range(seq_count):
            reward = rewards_ref[s]
            margin = margin + jnp.where(pairing_ref[i, 0] == s, reward, 0.0)
            margin = margin - jnp.where(pairing_ref[i, 1] == s, reward, 0.0)
        pair_weights.append(1.0 - jax.nn.sigmoid(jnp.full((1, LANES), margin, jnp.float32)))

    def project(c, total):
        for copy in loads(c):
            copy.wait()
        return total + jnp.dot(tokens[c], weights[c], preferred_element_type=jnp.float32)

    projected = lax.fori_loop(
        0, CHUNKS, project, jnp.zeros((2 * slots, 2 * half), jnp.float32)
    )

    token_lane = lax.broadcasted_iota(jnp.int32, (slots, LANES), 1)
    act = projected[:slots]
    act = jnp.where(token_lane < half, act, pltpu.roll(act, half, 1))
    grad = projected[slots:]
    grad = jnp.where(token_lane < half, pltpu.roll(grad, half, 1), grad)
    products = lax.dot_general(
        grad * signs, act, (((0,), (0,)), ((), ())),
        precision=lax.Precision.HIGHEST, preferred_element_type=jnp.float32,
    )
    for i in range(pair_count):
        outer_products[i * half:(i + 1) * half, :] = products[i * half:(i + 1) * half] * pair_weights[i]
    lines = pair_count * half // 2
    even = outer_products[pl.ds(0, lines, stride=2), :]
    odd = outer_products[pl.ds(1, lines, stride=2), :]
    flat_lane = lax.broadcasted_iota(jnp.int32, (lines, LANES), 1)
    flat = jnp.where(flat_lane < half, even, odd)
    for g in range(group):
        for i in range(pair_count):
            start = i * (half // 2) + g * rows
            train_send[g, i * rows:(i + 1) * rows, :] = flat[start:start + rows]

    def train(step):
        other, device = member(step)
        return remote(
            train_send.at[other], train_recv.at[mine], t_send, t_recv, device
        )

    repeat(1, group, lambda step: train(step).start())
    train_recv[mine] = train_send[mine]

    own.wait()
    queries_sent = all_of(query_all, q_send, q_recv)
    queries_sent.wait_recv()
    query_rows = query_all[...].astype(jnp.float32).reshape(-1, entries).astype(jnp.bfloat16)
    train_sent = all_of(train_recv, t_send, t_recv)
    train_sent.wait_recv()

    received = train_recv[...].reshape(group * pair_count, rows, LANES)
    left = jnp.concatenate([received[:, r, :] for r in range(rows)], axis=1).astype(jnp.bfloat16)
    partial = lax.dot_general(
        left, query_rows, (((1,), (1,)), ((), ())), preferred_element_type=jnp.float32
    )
    for g in range(group):
        part_send[g] = partial[g * pair_count:(g + 1) * pair_count]

    def scores(step):
        other, device = member(step)
        return remote(
            part_send.at[other], part_recv.at[mine], p_send, p_recv, device
        )

    repeat(1, group, lambda step: scores(step).start())
    kept = pltpu.make_async_copy(part_send.at[mine], part_recv.at[mine], own_sem)
    kept.start()
    scores_sent = all_of(part_recv, p_send, p_recv)
    queries_sent.wait_send()
    train_sent.wait_send()
    scores_sent.wait_send()
    scores_sent.wait_recv()
    kept.wait()


def solution(mesh):
    devices = mesh.shape["dp"]
    inner = math.gcd(devices, 8)
    outer = 1
    reps = devices // (inner * outer)
    group = outer * inner

    def local(activations, out_grads, projectors, rewards, lengths, pairing, queries):
        slots, width = activations.shape[1:]
        half = projectors.shape[2] // 2
        pair_count = pairing.shape[0]
        per_device, length = queries.shape[1:]
        entries = length // group
        rows = pair_count * entries // LANES
        dma = lambda *shape: pltpu.SemaphoreType.DMA(shape) if shape else pltpu.SemaphoreType.DMA
        hbm = pl.BlockSpec(memory_space=pltpu.HBM)
        partial_scores = pl.pallas_call(
            functools.partial(kernel, outer, reps, inner),
            out_shape=jax.ShapeDtypeStruct((group, pair_count, devices * per_device), jnp.float32),
            in_specs=[hbm] * 7,
            out_specs=hbm,
            scratch_shapes=[
                pltpu.VMEM((CHUNKS, 2 * slots, width // CHUNKS), jnp.bfloat16),
                pltpu.VMEM((CHUNKS, width // CHUNKS, 2 * half), jnp.bfloat16),
                pltpu.VMEM((devices, per_device, entries), jnp.bfloat16),
                pltpu.VMEM((pair_count * half, LANES), jnp.float32),
                pltpu.VMEM((group, rows, LANES), jnp.float32),
                pltpu.VMEM((group, rows, LANES), jnp.float32),
                pltpu.VMEM((group, pair_count, devices * per_device), jnp.float32),
                pltpu.SMEM(rewards.shape, rewards.dtype),
                pltpu.SMEM(lengths.shape, lengths.dtype),
                pltpu.SMEM(pairing.shape, pairing.dtype),
                dma(3), dma(CHUNKS, 3), dma(), dma(), dma(), dma(), dma(), dma(), dma(),
            ],
            compiler_params=pltpu.CompilerParams(
                collective_id=0, has_side_effects=True, vmem_limit_bytes=56 * 1024 * 1024
            ),
        )(activations, out_grads, projectors, rewards, lengths, pairing, queries)
        return lax.psum_scatter(partial_scores.sum(axis=0), "layer", scatter_dimension=1, tiled=True)

    return jax.shard_map(
        local,
        mesh=mesh,
        in_specs=(
            P("layer", "dp", None),
            P("layer", "dp", None),
            P("layer", None, None),
            P("dp"),
            P("dp"),
            P("dp", None),
            P("layer", "dp", None),
        ),
        out_specs=P("dp", "layer"),
        check_vma=False,
    )
```

```python
import functools
import math

import jax
import jax.numpy as jnp
from jax import lax
from jax.experimental import pallas as pl
from jax.experimental.pallas import tpu as pltpu
from jax.sharding import PartitionSpec as P

LANES = 128
CHUNKS = 4


def kernel(
    outer, reps, inner,
    act_ref, grad_ref, proj_ref, rewards_hbm, lengths_hbm, pairing_hbm, queries_ref, part_recv,
    tokens, weights, query_all, outer_products, train_send, train_recv, part_send,
    rewards_ref, lengths_ref, pairing_ref, small_sem, load_sem, own_sem, q_send, q_recv, t_send, t_recv, p_send, p_recv,
):
    group = outer * inner
    me = lax.axis_index("dp")
    place = me % inner
    rep = (me // inner) % reps
    slab = me // (inner * reps)
    mine = slab * inner + place
    slots, width = act_ref.shape[1], act_ref.shape[2]
    seq_count = lengths_hbm.shape[0]
    seq_len = slots // seq_count
    half = proj_ref.shape[2] // 2
    pair_count = pairing_hbm.shape[0]
    entries = queries_ref.shape[2] // group
    rows = entries // LANES

    def member(step):
        other = lax.rem(mine + step, group)
        return other, (other // inner * reps + rep) * inner + lax.rem(other, inner)

    def stranger(step):
        device = lax.rem(me + step, outer * reps * inner)
        return device // (inner * reps) * inner + lax.rem(device, inner), device

    def repeat(low, high, body):
        lax.fori_loop(low, high, lambda step, carry: (body(step), carry)[1], 0)

    part = width // CHUNKS

    def loads(c):
        cols = pl.ds(pl.multiple_of(c * part, LANES), part)
        return (
            pltpu.make_async_copy(proj_ref.at[0, cols, :], weights.at[c], load_sem.at[c, 0]),
            pltpu.make_async_copy(
                act_ref.at[0, :, cols], tokens.at[c, pl.ds(0, slots), :], load_sem.at[c, 1]
            ),
            pltpu.make_async_copy(
                grad_ref.at[0, :, cols], tokens.at[c, pl.ds(slots, slots), :], load_sem.at[c, 2]
            ),
        )

    def start_loads(c):
        for copy in loads(c):
            copy.start()

    barrier = pltpu.get_barrier_semaphore()

    def greet(device):
        pl.semaphore_signal(
            barrier, inc=1, device_id={"dp": device}, device_id_type=pl.DeviceIdType.MESH
        )

    devices = outer * reps * inner
    repeat(0, CHUNKS, start_loads)
    repeat(1, devices, lambda step: greet(stranger(step)[1]))

    def chunk_of(index):
        return queries_ref.at[0, :, pl.ds(pl.multiple_of(index * entries, LANES), entries)]

    own = pltpu.make_async_copy(chunk_of(mine), query_all.at[me], own_sem)
    own.start()
    small = [
        pltpu.make_async_copy(rewards_hbm, rewards_ref, small_sem.at[0]),
        pltpu.make_async_copy(lengths_hbm, lengths_ref, small_sem.at[1]),
        pltpu.make_async_copy(pairing_hbm, pairing_ref, small_sem.at[2]),
    ]
    for copy in small:
        copy.start()
    pl.semaphore_wait(barrier, devices - 1)

    def remote(src, dst, send_sem, recv_sem, device):
        return pltpu.make_async_remote_copy(
            src_ref=src, dst_ref=dst, send_sem=send_sem, recv_sem=recv_sem,
            device_id={"dp": device}, device_id_type=pl.DeviceIdType.MESH,
        )

    def all_of(ref, send_sem, recv_sem):
        blocks = ref.at[pl.ds(0, ref.shape[0] - 1)]
        return remote(blocks, blocks, send_sem, recv_sem, stranger(1)[1])

    def query(step):
        other, device = stranger(step)
        return remote(
            chunk_of(other), query_all.at[me], q_send, q_recv, device
        )

    repeat(0, devices - 1, lambda turn: query(lax.rem(turn + group - 1, devices - 1) + 1).start())

    for copy in small:
        copy.wait()
    lane = lax.broadcasted_iota(jnp.int32, (seq_len, LANES), 1)
    spot = lax.broadcasted_iota(jnp.int32, (seq_len, LANES), 0)
    signs = []
    for s in range(seq_count):
        sign = []
        for i in range(pair_count):
            is_chosen = (pairing_ref[i, 0] == s).astype(jnp.float32)
            is_rejected = (pairing_ref[i, 1] == s).astype(jnp.float32)
            sign.append(is_rejected - is_chosen)
        both = jnp.where(lane < half, sign[0], sign[1])
        signs.append(jnp.where(spot < lengths_ref[s], both, 0.0))
    signs = jnp.concatenate(signs, axis=0)
    pair_weights = []
    for i in range(pair_count):
        margin = jnp.float32(0.0)
        for s in range(seq_count):
            reward = rewards_ref[s]
            margin = margin + jnp.where(pairing_ref[i, 0] == s, reward, 0.0)
            margin = margin - jnp.where(pairing_ref[i, 1] == s, reward, 0.0)
        pair_weights.append(1.0 - jax.nn.sigmoid(jnp.full((1, LANES), margin, jnp.float32)))

    def project(c, total):
        for copy in loads(c):
            copy.wait()
        return total + jnp.dot(tokens[c], weights[c], preferred_element_type=jnp.float32)

    projected = lax.fori_loop(
        0, CHUNKS, project, jnp.zeros((2 * slots, 2 * half), jnp.float32)
    )

    token_lane = lax.broadcasted_iota(jnp.int32, (slots, LANES), 1)
    act = projected[:slots]
    act = jnp.where(token_lane < half, act, pltpu.roll(act, half, 1))
    grad = projected[slots:]
    grad = jnp.where(token_lane < half, pltpu.roll(grad, half, 1), grad)
    products = lax.dot_general(
        grad * signs, act, (((0,), (0,)), ((), ())),
        precision=lax.Precision.HIGHEST, preferred_element_type=jnp.float32,
    )
    for i in range(pair_count):
        outer_products[i * half:(i + 1) * half, :] = products[i * half:(i + 1) * half] * pair_weights[i]
    lines = pair_count * half // 2
    even = outer_products[pl.ds(0, lines, stride=2), :]
    odd = outer_products[pl.ds(1, lines, stride=2), :]
    flat_lane = lax.broadcasted_iota(jnp.int32, (lines, LANES), 1)
    flat = jnp.where(flat_lane < half, even, odd)
    for g in range(group):
        for i in range(pair_count):
            start = i * (half // 2) + g * rows
            train_send[g, i * rows:(i + 1) * rows, :] = flat[start:start + rows]

    def train(step):
        other, device = member(step)
        return remote(
            train_send.at[other], train_recv.at[mine], t_send, t_recv, device
        )

    repeat(1, group, lambda step: train(step).start())
    train_recv[mine] = train_send[mine]

    own.wait()
    queries_sent = all_of(query_all, q_send, q_recv)
    queries_sent.wait_recv()
    query_rows = query_all[...].astype(jnp.float32).reshape(-1, entries).astype(jnp.bfloat16)
    train_sent = all_of(train_recv, t_send, t_recv)
    train_sent.wait_recv()

    received = train_recv[...].reshape(group * pair_count, rows, LANES)
    left = jnp.concatenate([received[:, r, :] for r in range(rows)], axis=1).astype(jnp.bfloat16)
    partial = lax.dot_general(
        left, query_rows, (((1,), (1,)), ((), ())), preferred_element_type=jnp.float32
    )
    for g in range(group):
        part_send[g] = partial[g * pair_count:(g + 1) * pair_count]

    def scores(step):
        other, device = member(step)
        return remote(
            part_send.at[other], part_recv.at[mine], p_send, p_recv, device
        )

    repeat(1, group, lambda step: scores(step).start())
    kept = pltpu.make_async_copy(part_send.at[mine], part_recv.at[mine], own_sem)
    kept.start()
    scores_sent = all_of(part_recv, p_send, p_recv)
    queries_sent.wait_send()
    train_sent.wait_send()
    scores_sent.wait_send()
    scores_sent.wait_recv()
    kept.wait()


def solution(mesh):
    devices = mesh.shape["dp"]
    inner = math.gcd(devices, 8)
    outer = 1
    reps = devices // (inner * outer)
    group = outer * inner

    def local(activations, out_grads, projectors, rewards, lengths, pairing, queries):
        slots, width = activations.shape[1:]
        half = projectors.shape[2] // 2
        pair_count = pairing.shape[0]
        per_device, length = queries.shape[1:]
        entries = length // group
        rows = pair_count * entries // LANES
        dma = lambda *shape: pltpu.SemaphoreType.DMA(shape) if shape else pltpu.SemaphoreType.DMA
        hbm = pl.BlockSpec(memory_space=pltpu.HBM)
        partial_scores = pl.pallas_call(
            functools.partial(kernel, outer, reps, inner),
            out_shape=jax.ShapeDtypeStruct((group, pair_count, devices * per_device), jnp.float32),
            in_specs=[hbm] * 7,
            out_specs=hbm,
            scratch_shapes=[
                pltpu.VMEM((CHUNKS, 2 * slots, width // CHUNKS), jnp.bfloat16),
                pltpu.VMEM((CHUNKS, width // CHUNKS, 2 * half), jnp.bfloat16),
                pltpu.VMEM((devices, per_device, entries), jnp.bfloat16),
                pltpu.VMEM((pair_count * half, LANES), jnp.float32),
                pltpu.VMEM((group, rows, LANES), jnp.float32),
                pltpu.VMEM((group, rows, LANES), jnp.float32),
                pltpu.VMEM((group, pair_count, devices * per_device), jnp.float32),
                pltpu.SMEM(rewards.shape, rewards.dtype),
                pltpu.SMEM(lengths.shape, lengths.dtype),
                pltpu.SMEM(pairing.shape, pairing.dtype),
                dma(3), dma(CHUNKS, 3), dma(), dma(), dma(), dma(), dma(), dma(), dma(),
            ],
            compiler_params=pltpu.CompilerParams(
                collective_id=0, has_side_effects=True, vmem_limit_bytes=56 * 1024 * 1024
            ),
        )(activations, out_grads, projectors, rewards, lengths, pairing, queries)
        return lax.psum_scatter(partial_scores.sum(axis=0), "layer", scatter_dimension=1, tiled=True)

    return jax.shard_map(
        local,
        mesh=mesh,
        in_specs=(
            P("layer", "dp", None),
            P("layer", "dp", None),
            P("layer", None, None),
            P("dp"),
            P("dp"),
            P("dp", None),
            P("layer", "dp", None),
        ),
        out_specs=P("dp", "layer"),
        check_vma=False,
    )
```
